32 devices in a mesh: section: 8 (over y, x, core), batch: 4 (over z).
Axes of the slice: x: 2, y: 2, z: 4, core: 2. Of those that a mesh axis runs over, the one named last changes fastest.
Arguments:
- states: bfloat16 [16, 8, 64, 1024], P('section', 'batch'), may hold values from -6 to 6
- weights: bfloat16 [16, 64, 576], P('section'), may hold values from -0.25 to 0.25
- guess: float32 [8, 8, 64, 1024], P('section', 'batch'), may hold values from -6 to 6
- loss_cotangent: float32 [8, 64, 1024], P('batch'), may hold values from -6 to 6
Outputs:
- start_cotangents: float32 [8, 8, 64, 1024], P('section', 'batch')
- weight_grads: float32 [16, 36864], P('section', 'batch')
The draws below stay inside these ranges and needn't reach their ends.
All inputs are finite; a program needn't handle non-finite values.
Results may differ from the reference program's by a relative error of at most 0.0039.
Values may be sent and summed in bfloat16 or wider, within the bound.
A program may use at most 128 MiB of HBM per device.

```python
import math
import jax
import jax.numpy as jnp
from jax import lax

C = 64
SECTIONS = 8
LAYERS = 16
BATCH = 8
PIXELS = 1024


def block_scale(own_key, shape, cuts, least, top_value):
    level = 1.0
    for dim, shards_of in cuts:
        steps = jax.random.uniform(jax.random.fold_in(jax.random.fold_in(own_key, 6), dim), (shards_of,), jnp.float32, least / len(cuts), top_value / len(cuts))
        level = level * jnp.repeat(jnp.exp(steps), shape[dim] // shards_of).reshape((-1,) + (1,) * (len(shape) - 1 - dim))
    return level


def centred(own_key, extent, deviation, limit, shards=(), kind=jnp.bfloat16):
    values = deviation * jax.random.normal(own_key, extent, jnp.float32)
    if shards:
        values = values * block_scale(own_key, extent, shards, -0.22, 0.18)
    return jnp.clip(values, -limit, limit).astype(kind)


def setup_inputs(seed: int = 0) -> dict:
    arg_keys = jax.random.split(jax.random.key(seed), 5)
    return {
        "states": centred(arg_keys[0], (LAYERS, BATCH, C, PIXELS), 1.0, 6.0, ((0, 8), (1, 4))),
        "weights": centred(arg_keys[1], (LAYERS, C, 9 * C), (9 * C) ** -0.5, 0.25, ((0, 8),)),
        "guess": centred(arg_keys[2], (SECTIONS, BATCH, C, PIXELS), 1.0, 6.0, ((0, 8), (1, 4)), jnp.float32),
        "loss_cotangent": centred(arg_keys[3], (BATCH, C, PIXELS), 1.0, 6.0, ((0, 4),), jnp.float32),
    }


STEP = 0.0625

def unfold_taps(values, pixel_side, direction):
    length = values.shape[-1]
    margin = pixel_side + 1
    widths = [(0, 0)] * (values.ndim - 1) + [(margin, margin)]
    padded = jnp.pad(values, widths)
    column_base = jnp.arange(length) % pixel_side
    copies = []
    for row_step in (-1, 0, 1):
        for col_step in (-1, 0, 1):
            delta = direction * (row_step * pixel_side + col_step)
            window = lax.slice_in_dim(padded, margin + delta, margin + delta + length, axis=values.ndim - 1)
            column = column_base + direction * col_step
            inside = (column >= 0) & (column < pixel_side)
            copies.append(jnp.where(inside, window, jnp.zeros_like(window)))
    return jnp.stack(copies, axis=1)

def back_conv(weight, rounded, pixel_side):
    channels = weight.shape[0]
    kernel = weight.reshape(channels, 9, channels).astype(jnp.float32)
    stacked = unfold_taps(rounded, pixel_side, -1).astype(jnp.float32)
    return jnp.einsum('okc,bkop->bcp', kernel, stacked)

def advance(cotangent, rounded, layer_state, weight, step_size, pixel_side):
    activ = jnp.tanh(layer_state.astype(jnp.float32))
    return cotangent + step_size * (1.0 - activ * activ) * back_conv(weight, rounded, pixel_side)

def layer_grad(rounded, layer_state, pixel_side):
    activ = jnp.tanh(layer_state.astype(jnp.float32)).astype(jnp.bfloat16)
    stacked = unfold_taps(activ, pixel_side, 1).astype(jnp.float32)
    return (jnp.einsum('bop,bkcp->okc', rounded.astype(jnp.float32), stacked) * STEP).reshape(-1)

def reference(states, weights, guess, loss_cotangent):
    pixel_side = math.isqrt(states.shape[-1])
    sections = guess.shape[0]
    per_section = states.shape[0] // sections
    grouped_states = states.reshape((sections, per_section) + states.shape[1:])
    grouped_weights = weights.reshape((sections, per_section) + weights.shape[1:])

    def relax_section(packed):
        sec_states, sec_weights, initial = packed

        def fine_layer(cotangent, layer_pack):
            return (advance(cotangent, cotangent.astype(jnp.bfloat16), layer_pack[0], layer_pack[1], STEP, pixel_side), None)
        result, unused = lax.scan(fine_layer, initial, (sec_states, sec_weights), reverse=True)
        return result
    relaxed = lax.map(relax_section, (grouped_states, grouped_weights, guess))
    last_resid = (loss_cotangent - guess[-1])[None]
    residual = jnp.concatenate([relaxed[1:] - guess[:-1], last_resid], axis=0)

    def coarse_link(running, inputs):
        resid_row, first_state, first_weight = inputs
        value = advance(running, running.astype(jnp.bfloat16), first_state, first_weight, per_section * STEP, pixel_side) + resid_row
        return (value, value)
    unused, solved = lax.scan(coarse_link, residual[-1], (residual[:-1], grouped_states[1:, 0], grouped_weights[1:, 0]), reverse=True)
    correction = jnp.concatenate([solved, residual[-1:]], axis=0)
    new_guess = guess + correction

    def final_section(packed):
        sec_states, sec_weights, initial = packed

        def fine_layer(cotangent, layer_pack):
            layer_state, weight = layer_pack
            rounded = cotangent.astype(jnp.bfloat16)
            gradient = layer_grad(rounded, layer_state, pixel_side)
            return (advance(cotangent, rounded, layer_state, weight, STEP, pixel_side), gradient)
        result, gradients = lax.scan(fine_layer, initial, (sec_states, sec_weights), reverse=True)
        return (result, gradients)
    start_cot, gradients = lax.map(final_section, (grouped_states, grouped_weights, new_guess))
    return (start_cot, gradients.reshape(states.shape[0], -1))
```

```python
import functools
import math

import jax
import jax.numpy as jnp
from jax import lax
from jax.experimental import pallas as pl
from jax.experimental.pallas import tpu as pltpu
from jax.sharding import PartitionSpec as P

STEP = 0.0625
CHUNKS = 4
MESH = pl.DeviceIdType.MESH


def kernel(
    sections, groups, side,
    states_ref, weights_ref, guess_ref, loss_ref, start_ref, grads_ref,
    wide, blocks, scaled, held, base, incoming, outgoing, taps, acts, parts, landed,
    send_sem, recv_sem, part_send, part_recv,
):
    position = lax.axis_index("section")
    member = lax.axis_index("batch")
    layers = states_ref.shape[0]
    lanes, length = guess_ref.shape
    channels = weights_ref.shape[1]
    size = length // CHUNKS
    f32, bf16 = jnp.float32, jnp.bfloat16

    barrier = pltpu.get_barrier_semaphore()

    @pl.when(position > 0)
    def _():
        pl.semaphore_signal(
            barrier, inc=1, device_id={"section": position - 1}, device_id_type=MESH
        )

    @pl.when(position < sections - 1)
    def _():
        pl.semaphore_signal(
            barrier, inc=1, device_id={"section": position + 1}, device_id_type=MESH
        )

    for offset in range(1, groups):
        pl.semaphore_signal(
            barrier,
            inc=1,
            device_id={"batch": lax.rem(member + offset, groups)},
            device_id_type=MESH,
        )

    column = lax.broadcasted_iota(jnp.int32, (size, lanes), 0) % side
    not_first = column > 0
    not_last = column < side - 1
    low = lax.broadcasted_iota(jnp.int32, (channels, lanes), 1) < channels

    def shifted(values):
        before = jnp.where(not_first, pltpu.roll(values, 1, 0), 0.0)
        after = jnp.where(not_last, pltpu.roll(values, size - 1, 0), 0.0)
        return before.astype(bf16), values.astype(bf16), after.astype(bf16)

    def put_taps(first, values):
        before, same, after = shifted(values)
        rows = pl.ds(first + side, size)
        taps[rows, 0:lanes] = after
        taps[rows, lanes : 2 * lanes] = same
        taps[rows, 2 * lanes : 3 * lanes] = before

    def conv(layer, first):
        stacked = jnp.concatenate(
            [taps[pl.ds(first + side - a * side, size), :] for a in (-1, 0, 1)], axis=1
        )
        return jnp.dot(stacked, blocks[layer], preferred_element_type=f32)

    def prepare_weights(layer):
        wide[:, 9 * channels :] = jnp.zeros((channels, wide.shape[1] - 9 * channels), f32)
        wide[:, 0 : 9 * channels] = weights_ref[layer].astype(f32)
        for k in range(9):
            pair = wide[:, (k // 2) * lanes : (k // 2 + 1) * lanes]
            turned = pltpu.roll(pair, channels, 1)
            left, right = (pair, turned) if k % 2 == 0 else (turned, pair)
            blocks[layer, k * lanes : k * lanes + channels, :] = jnp.where(
                low, left, 0.0
            ).astype(bf16)
            blocks[layer, k * lanes + channels : (k + 1) * lanes, :] = jnp.where(
                low, 0.0, right
            ).astype(bf16)

    def prepare_state(layer):
        activ = jnp.tanh(states_ref[layer].astype(f32)).T
        scaled[layer] = STEP * (1.0 - activ * activ)
        edge = jnp.zeros((side, 3 * lanes), bf16)
        acts[layer, 0:side, :] = edge
        acts[layer, side + length :, :] = edge
        for i in range(CHUNKS):
            before, same, after = shifted(activ[i * size : (i + 1) * size])
            rows = slice(side + i * size, side + (i + 1) * size)
            acts[layer, rows, 0:lanes] = before
            acts[layer, rows, lanes : 2 * lanes] = same
            acts[layer, rows, 2 * lanes :] = after

    edge = jnp.zeros((side, 3 * lanes), bf16)
    taps[0:side, :] = edge
    taps[side + length :, :] = edge
    for layer in range(layers):
        prepare_weights(layer)
        prepare_state(layer)

    @pl.when(position == sections - 1)
    def _():
        incoming[...] = loss_ref[...].T

    held[...] = guess_ref[...].T

    base[...] = jnp.zeros_like(base)
    for layer in range(layers - 1, -1, -1):
        for i in range(CHUNKS):
            rows = slice(i * size, (i + 1) * size)
            put_taps(i * size, held[rows, :] + base[rows, :])
        for i in range(CHUNKS):
            rows = slice(i * size, (i + 1) * size)
            base[rows, :] += scaled[layer, rows, :] * conv(layer, i * size)

    neighbours = (
        groups - 1
        + (position > 0).astype(jnp.int32)
        + (position < sections - 1).astype(jnp.int32)
    )
    pl.semaphore_wait(barrier, neighbours)

    def hop(i):
        rows = pl.ds(i * size, size)
        return pltpu.make_async_remote_copy(
            src_ref=outgoing.at[rows, :],
            dst_ref=incoming.at[rows, :],
            send_sem=send_sem.at[i],
            recv_sem=recv_sem.at[i],
            device_id={"section": position - 1},
            device_id_type=MESH,
        )

    def carry(i):
        rows = slice(i * size, (i + 1) * size)
        outgoing[rows, :] = (
            incoming[rows, :] + base[rows, :]
            + layers * scaled[0, rows, :] * conv(0, i * size)
        )
        hop(i).start()

    for i in range(CHUNKS):
        @pl.when(position < sections - 1)
        def _():
            hop(i).wait_recv()

        @pl.when(position > 0)
        def _():
            rows = slice(i * size, (i + 1) * size)
            put_taps(i * size, incoming[rows, :] - held[rows, :])
            if i > 0:
                carry(i - 1)

    @pl.when(position > 0)
    def _():
        carry(CHUNKS - 1)

    def share(layer, offset):
        peer = lax.rem(member + offset, groups)
        return pltpu.make_async_remote_copy(
            src_ref=parts.at[layer, peer],
            dst_ref=landed.at[layer, offset - 1],
            send_sem=part_send.at[layer, offset - 1],
            recv_sem=part_recv.at[layer, offset - 1],
            device_id={"batch": peer},
            device_id_type=MESH,
        )

    for layer in range(layers - 1, -1, -1):
        turned_lam = incoming[...].T.astype(bf16)
        sums = []
        for a in (-1, 0, 1):
            first = side + a * side
            sums.append(
                jnp.dot(
                    turned_lam,
                    acts[layer, first : first + length, :],
                    preferred_element_type=f32,
                )
            )
        pieces = [sums[k // 3][:, (k % 3) * lanes : (k % 3 + 1) * lanes] for k in range(9)]
        held_rows = channels // groups
        for k in range(0, 9, 2):
            even = pieces[k][:channels] + pltpu.roll(pieces[k][channels:], channels, 1)
            if k < 8:
                odd = pltpu.roll(pieces[k + 1][:channels], channels, 1) + pieces[k + 1][channels:]
                both = jnp.where(low, even, odd) * STEP
                width = lanes
            else:
                both = even[:, :channels] * STEP
                width = channels
            for g in range(groups):
                parts[layer, g, :, k * channels : k * channels + width] = both[
                    g * held_rows : (g + 1) * held_rows
                ]
        for offset in range(1, groups):
            share(layer, offset).start()

        for i in range(CHUNKS):
            put_taps(i * size, incoming[i * size : (i + 1) * size, :])
        for i in range(CHUNKS):
            rows = slice(i * size, (i + 1) * size)
            incoming[rows, :] += scaled[layer, rows, :] * conv(layer, i * size)

    start_ref[...] = incoming[...].T

    for layer in range(layers - 1, -1, -1):
        total = parts[layer, member]
        for offset in range(1, groups):
            share(layer, offset).wait_recv()
            total = total + landed[layer, offset - 1]
        grads_ref[layer] = total
        for offset in range(1, groups):
            share(layer, offset).wait_send()

    @pl.when(position > 0)
    def _():
        for i in range(CHUNKS):
            hop(i).wait_send()


def shards(states, weights, guess, loss_cotangent):
    sections = lax.axis_size("section")
    groups = lax.axis_size("batch")
    layers, images, channels, length = states.shape
    side = math.isqrt(length)
    lanes = images * channels
    rows = channels // groups
    f32, bf16 = jnp.float32, jnp.bfloat16
    start, grads = pl.pallas_call(
        functools.partial(kernel, sections, groups, side),
        out_shape=(
            jax.ShapeDtypeStruct((lanes, length), f32),
            jax.ShapeDtypeStruct((layers, rows, 9 * channels), f32),
        ),
        in_specs=[pl.BlockSpec(memory_space=pltpu.VMEM)] * 4,
        out_specs=(pl.BlockSpec(memory_space=pltpu.VMEM),) * 2,
        scratch_shapes=[
            pltpu.VMEM((channels, 5 * lanes), f32),
            pltpu.VMEM((layers, 9 * lanes, lanes), bf16),
            pltpu.VMEM((layers, length, lanes), f32),
            pltpu.VMEM((length, lanes), f32),
            pltpu.VMEM((length, lanes), f32),
            pltpu.VMEM((length, lanes), f32),
            pltpu.VMEM((length, lanes), f32),
            pltpu.VMEM((length + 2 * side, 3 * lanes), bf16),
            pltpu.VMEM((layers, length + 2 * side, 3 * lanes), bf16),
            pltpu.VMEM((layers, groups, rows, 9 * channels), f32),
            pltpu.VMEM((layers, groups - 1, rows, 9 * channels), f32),
            pltpu.SemaphoreType.DMA((CHUNKS,)),
            pltpu.SemaphoreType.DMA((CHUNKS,)),
            pltpu.SemaphoreType.DMA((layers, groups - 1)),
            pltpu.SemaphoreType.DMA((layers, groups - 1)),
        ],
        compiler_params=pltpu.CompilerParams(
            collective_id=0, has_side_effects=True, vmem_limit_bytes=40 * 2**20
        ),
    )(
        states.reshape(layers, lanes, length),
        weights,
        guess.reshape(lanes, length),
        loss_cotangent.reshape(lanes, length),
    )
    return start.reshape(guess.shape), grads.reshape(layers, rows * 9 * channels)


def solution(mesh):
    placed = (
        P("section", "batch", None, None),
        P("section", None, None),
        P("section", "batch", None, None),
        P("batch", None, None),
    )
    return jax.shard_map(
        shards,
        mesh=mesh,
        in_specs=placed,
        out_specs=(P("section", "batch", None, None), P("section", "batch")),
        check_vma=False,
    )
```

```python
import functools
import math

import jax
import jax.numpy as jnp
from jax import lax
from jax.experimental import pallas as pl
from jax.experimental.pallas import tpu as pltpu
from jax.sharding import PartitionSpec as P

STEP = 0.0625
PIECES = 4
CHUNKS = 8
FLYING = 2
MESH = pl.DeviceIdType.MESH


def kernel(
    sections, groups, side,
    states_hbm, weights_hbm, guess_hbm, loss_hbm, start_ref, grads_ref,
    states_ref, weights_ref, guess_ref, loss_ref,
    wide, blocks, scaled, held, base, incoming, outgoing, taps, acts, parts, sent, landed,
    send_sem, recv_sem, part_send, part_recv, load_sem,
):
    position = lax.axis_index("section")
    member = lax.axis_index("batch")
    layers = states_ref.shape[0]
    lanes, length = guess_ref.shape
    channels = weights_ref.shape[1]
    size, part = length // CHUNKS, length // PIECES
    f32, bf16 = jnp.float32, jnp.bfloat16

    loads = [
        pltpu.make_async_copy(source, target, load_sem.at[n])
        for n, (source, target) in enumerate(
            ((weights_hbm, weights_ref), (states_hbm, states_ref),
             (guess_hbm, guess_ref), (loss_hbm, loss_ref))
        )
    ]
    for load in loads:
        load.start()

    barrier = pltpu.get_barrier_semaphore()

    @pl.when(position > 0)
    def _():
        pl.semaphore_signal(
            barrier, inc=1, device_id={"section": position - 1}, device_id_type=MESH
        )

    @pl.when(position < sections - 1)
    def _():
        pl.semaphore_signal(
            barrier, inc=1, device_id={"section": position + 1}, device_id_type=MESH
        )

    for offset in range(1, groups):
        pl.semaphore_signal(
            barrier,
            inc=1,
            device_id={"batch": lax.rem(member + offset, groups)},
            device_id_type=MESH,
        )

    column = lax.broadcasted_iota(jnp.int32, (part, lanes), 0) % side
    not_first = column > 0
    not_last = column < side - 1
    low = lax.broadcasted_iota(jnp.int32, (channels, lanes), 1) < channels

    def shifted(values):
        count = values.shape[0]
        before = jnp.where(not_first[:count], pltpu.roll(values, 1, 0), 0.0)
        after = jnp.where(not_last[:count], pltpu.roll(values, count - 1, 0), 0.0)
        return before.astype(bf16), values.astype(bf16), after.astype(bf16)

    def put_taps(first, values):
        before, same, after = shifted(values)
        rows = pl.ds(first + side, values.shape[0])
        taps[rows, 0:lanes] = after
        taps[rows, lanes : 2 * lanes] = same
        taps[rows, 2 * lanes : 3 * lanes] = before

    def conv(layer, first, count):
        stacked = jnp.concatenate(
            [taps[pl.ds(first + side - a * side, count), :] for a in (-1, 0, 1)], axis=1
        )
        return jnp.dot(stacked, blocks[layer], preferred_element_type=f32)

    def prepare_weights(layer):
        wide[:, 9 * channels :] = jnp.zeros((channels, wide.shape[1] - 9 * channels), f32)
        wide[:, 0 : 9 * channels] = weights_ref[layer].astype(f32)
        for k in range(9):
            pair = wide[:, (k // 2) * lanes : (k // 2 + 1) * lanes]
            turned = pltpu.roll(pair, channels, 1)
            left, right = (pair, turned) if k % 2 == 0 else (turned, pair)
            blocks[layer, k * lanes : k * lanes + channels, :] = jnp.where(
                low, left, 0.0
            ).astype(bf16)
            blocks[layer, k * lanes + channels : (k + 1) * lanes, :] = jnp.where(
                low, 0.0, right
            ).astype(bf16)

    def prepare_state(layer):
        activ = jnp.tanh(states_ref[layer].astype(f32)).T
        scaled[layer] = STEP * (1.0 - activ * activ)

    def prepare_acts(layer):
        activ = jnp.tanh(states_ref[layer].astype(f32)).T
        edge = jnp.zeros((side, 3 * lanes), bf16)
        acts[layer, 0:side, :] = edge
        acts[layer, side + length :, :] = edge
        for i in range(PIECES):
            before, same, after = shifted(activ[i * part : (i + 1) * part])
            rows = slice(side + i * part, side + (i + 1) * part)
            acts[layer, rows, 0:lanes] = before
            acts[layer, rows, lanes : 2 * lanes] = same
            acts[layer, rows, 2 * lanes :] = after

    edge = jnp.zeros((side, 3 * lanes), bf16)
    taps[0:side, :] = edge
    taps[side + length :, :] = edge
    loads[0].wait()
    for layer in range(layers):
        prepare_weights(layer)
    loads[1].wait()
    for layer in range(layers):
        prepare_state(layer)
    loads[2].wait()
    loads[3].wait()

    @pl.when(position == sections - 1)
    def _():
        incoming[...] = loss_ref[...].T

    held[...] = guess_ref[...].T

    base[...] = jnp.zeros_like(base)
    for layer in range(layers - 1, -1, -1):
        for i in range(PIECES):
            rows = slice(i * part, (i + 1) * part)
            put_taps(i * part, held[rows, :] + base[rows, :])
        for i in range(PIECES):
            rows = slice(i * part, (i + 1) * part)
            base[rows, :] += scaled[layer, rows, :] * conv(layer, i * part, part)

    @pl.when(position < sections - 1)
    def _():
        for layer in range(layers):
            prepare_acts(layer)

    neighbours = (
        groups - 1
        + (position > 0).astype(jnp.int32)
        + (position < sections - 1).astype(jnp.int32)
    )
    pl.semaphore_wait(barrier, neighbours)

    def hop(i):
        rows = pl.ds(i * size, size)
        return pltpu.make_async_remote_copy(
            src_ref=outgoing.at[rows, :],
            dst_ref=incoming.at[rows, :],
            send_sem=send_sem.at[i],
            recv_sem=recv_sem.at[i],
            device_id={"section": position - 1},
            device_id_type=MESH,
        )

    def carry(i):
        rows = slice(i * size, (i + 1) * size)
        outgoing[rows, :] = (
            incoming[rows, :] + base[rows, :]
            + layers * scaled[0, rows, :] * conv(0, i * size, size)
        )
        if i >= FLYING:
            hop(i - FLYING).wait_send()
        hop(i).start()

    for i in range(CHUNKS):
        @pl.when(position < sections - 1)
        def _():
            hop(i).wait_recv()

        @pl.when(position > 0)
        def _():
            rows = slice(i * size, (i + 1) * size)
            put_taps(i * size, incoming[rows, :] - held[rows, :])
            if i > 0:
                carry(i - 1)

    @pl.when(position > 0)
    def _():
        carry(CHUNKS - 1)

    @pl.when(position == sections - 1)
    def _():
        for layer in range(layers):
            prepare_acts(layer)

    def share(layer, offset):
        peer = lax.rem(member + offset, groups)
        return pltpu.make_async_remote_copy(
            src_ref=sent.at[layer, peer],
            dst_ref=landed.at[layer, offset - 1],
            send_sem=part_send.at[layer, offset - 1],
            recv_sem=part_recv.at[layer, offset - 1],
            device_id={"batch": peer},
            device_id_type=MESH,
        )

    for layer in range(layers - 1, -1, -1):
        turned_lam = incoming[...].T.astype(bf16)
        sums = []
        for a in (-1, 0, 1):
            first = side + a * side
            sums.append(
                jnp.dot(
                    turned_lam,
                    acts[layer, first : first + length, :],
                    preferred_element_type=f32,
                )
            )
        pieces = [sums[k // 3][:, (k % 3) * lanes : (k % 3 + 1) * lanes] for k in range(9)]
        held_rows = channels // groups
        for k in range(0, 9, 2):
            even = pieces[k][:channels] + pltpu.roll(pieces[k][channels:], channels, 1)
            if k < 8:
                odd = pltpu.roll(pieces[k + 1][:channels], channels, 1) + pieces[k + 1][channels:]
                both = jnp.where(low, even, odd) * STEP
                width = lanes
            else:
                both = even[:, :channels] * STEP
                width = channels
            for g in range(groups):
                share_of = both[g * held_rows : (g + 1) * held_rows]
                columns = slice(k * channels, k * channels + width)
                parts[layer, g, :, columns] = share_of
                sent[layer, g, :, columns] = share_of.astype(bf16)
        for offset in range(1, groups):
            share(layer, offset).start()

        for i in range(PIECES):
            put_taps(i * part, incoming[i * part : (i + 1) * part, :])
        for i in range(PIECES):
            rows = slice(i * part, (i + 1) * part)
            incoming[rows, :] += scaled[layer, rows, :] * conv(layer, i * part, part)

    start_ref[...] = incoming[...].T

    for layer in range(layers - 1, -1, -1):
        total = parts[layer, member]
        for offset in range(1, groups):
            share(layer, offset).wait_recv()
            total = total + landed[layer, offset - 1].astype(f32)
        grads_ref[layer] = total
        for offset in range(1, groups):
            share(layer, offset).wait_send()

    @pl.when(position > 0)
    def _():
        for i in range(CHUNKS - FLYING, CHUNKS):
            hop(i).wait_send()


def shards(states, weights, guess, loss_cotangent):
    sections = lax.axis_size("section")
    groups = lax.axis_size("batch")
    layers, images, channels, length = states.shape
    side = math.isqrt(length)
    lanes = images * channels
    rows = channels // groups
    f32, bf16 = jnp.float32, jnp.bfloat16
    start, grads = pl.pallas_call(
        functools.partial(kernel, sections, groups, side),
        out_shape=(
            jax.ShapeDtypeStruct((lanes, length), f32),
            jax.ShapeDtypeStruct((layers, rows, 9 * channels), f32),
        ),
        in_specs=[pl.BlockSpec(memory_space=pltpu.HBM)] * 4,
        out_specs=(pl.BlockSpec(memory_space=pltpu.VMEM),) * 2,
        scratch_shapes=[
            pltpu.VMEM((layers, lanes, length), states.dtype),
            pltpu.VMEM(weights.shape, weights.dtype),
            pltpu.VMEM((lanes, length), f32),
            pltpu.VMEM((lanes, length), f32),
            pltpu.VMEM((channels, 5 * lanes), f32),
            pltpu.VMEM((layers, 9 * lanes, lanes), bf16),
            pltpu.VMEM((layers, length, lanes), f32),
            pltpu.VMEM((length, lanes), f32),
            pltpu.VMEM((length, lanes), f32),
            pltpu.VMEM((length, lanes), f32),
            pltpu.VMEM((length, lanes), f32),
            pltpu.VMEM((length + 2 * side, 3 * lanes), bf16),
            pltpu.VMEM((layers, length + 2 * side, 3 * lanes), bf16),
            pltpu.VMEM((layers, groups, rows, 9 * channels), f32),
            pltpu.VMEM((layers, groups, rows, 9 * channels), bf16),
            pltpu.VMEM((layers, groups - 1, rows, 9 * channels), bf16),
            pltpu.SemaphoreType.DMA((CHUNKS,)),
            pltpu.SemaphoreType.DMA((CHUNKS,)),
            pltpu.SemaphoreType.DMA((layers, groups - 1)),
            pltpu.SemaphoreType.DMA((layers, groups - 1)),
            pltpu.SemaphoreType.DMA((4,)),
        ],
        compiler_params=pltpu.CompilerParams(
            collective_id=0, has_side_effects=True, vmem_limit_bytes=40 * 2**20
        ),
    )(
        states.reshape(layers, lanes, length),
        weights,
        guess.reshape(lanes, length),
        loss_cotangent.reshape(lanes, length),
    )
    return start.reshape(guess.shape), grads.reshape(layers, rows * 9 * channels)


def solution(mesh):
    placed = (
        P("section", "batch", None, None),
        P("section", None, None),
        P("section", "batch", None, None),
        P("batch", None, None),
    )
    return jax.shard_map(
        shards,
        mesh=mesh,
        in_specs=placed,
        out_specs=(P("section", "batch", None, None), P("section", "batch")),
        check_vma=False,
    )
```

```python
import functools
import math

import jax
import jax.numpy as jnp
from jax import lax
from jax.experimental import pallas as pl
from jax.experimental.pallas import tpu as pltpu
from jax.sharding import PartitionSpec as P

STEP = 0.0625
PIECES = 4
CHUNKS = 8
FLYING = 2
MESH = pl.DeviceIdType.MESH


def kernel(
    sections, groups, side,
    states_hbm, weights_hbm, guess_hbm, loss_hbm, start_ref, grads_ref,
    states_ref, weights_ref, guess_ref, loss_ref,
    wide, blocks, scaled, held, base, incoming, outgoing, taps, acts, parts, sent, landed,
    send_sem, recv_sem, part_send, part_recv, load_sem,
):
    position = lax.axis_index("section")
    member = lax.axis_index("batch")
    layers = states_ref.shape[0]
    lanes, length = guess_ref.shape
    channels = weights_ref.shape[1]
    size, part = length // CHUNKS, length // PIECES
    f32, bf16 = jnp.float32, jnp.bfloat16

    loads = [
        pltpu.make_async_copy(source, target, load_sem.at[n])
        for n, (source, target) in enumerate(
            ((weights_hbm, weights_ref), (states_hbm, states_ref),
             (guess_hbm, guess_ref), (loss_hbm, loss_ref))
        )
    ]
    for load in loads:
        load.start()

    barrier = pltpu.get_barrier_semaphore()

    @pl.when(position > 0)
    def _():
        pl.semaphore_signal(
            barrier, inc=1, device_id={"section": position - 1}, device_id_type=MESH
        )

    @pl.when(position < sections - 1)
    def _():
        pl.semaphore_signal(
            barrier, inc=1, device_id={"section": position + 1}, device_id_type=MESH
        )

    for offset in range(1, groups):
        pl.semaphore_signal(
            barrier,
            inc=1,
            device_id={"batch": lax.rem(member + offset, groups)},
            device_id_type=MESH,
        )

    column = lax.broadcasted_iota(jnp.int32, (part, lanes), 0) % side
    not_first = column > 0
    not_last = column < side - 1
    low = lax.broadcasted_iota(jnp.int32, (channels, lanes), 1) < channels

    def shifted(values):
        count = values.shape[0]
        before = jnp.where(not_first[:count], pltpu.roll(values, 1, 0), 0.0)
        after = jnp.where(not_last[:count], pltpu.roll(values, count - 1, 0), 0.0)
        return before.astype(bf16), values.astype(bf16), after.astype(bf16)

    def put_taps(first, values):
        before, same, after = shifted(values)
        rows = pl.ds(first + side, values.shape[0])
        taps[rows, 0:lanes] = after
        taps[rows, lanes : 2 * lanes] = same
        taps[rows, 2 * lanes : 3 * lanes] = before

    def conv(layer, first, count):
        stacked = jnp.concatenate(
            [taps[pl.ds(first + side - a * side, count), :] for a in (-1, 0, 1)], axis=1
        )
        return jnp.dot(stacked, blocks[layer], preferred_element_type=f32)

    def prepare_weights(layer):
        wide[:, 9 * channels :] = jnp.zeros((channels, wide.shape[1] - 9 * channels), f32)
        wide[:, 0 : 9 * channels] = weights_ref[layer].astype(f32)
        for k in range(9):
            pair = wide[:, (k // 2) * lanes : (k // 2 + 1) * lanes]
            turned = pltpu.roll(pair, channels, 1)
            left, right = (pair, turned) if k % 2 == 0 else (turned, pair)
            blocks[layer, k * lanes : k * lanes + channels, :] = jnp.where(
                low, left, 0.0
            ).astype(bf16)
            blocks[layer, k * lanes + channels : (k + 1) * lanes, :] = jnp.where(
                low, 0.0, right
            ).astype(bf16)

    def prepare_state(layer):
        activ = jnp.tanh(states_ref[layer].astype(f32)).T
        scaled[layer] = STEP * (1.0 - activ * activ)

    def prepare_acts(layer):
        activ = jnp.tanh(states_ref[layer].astype(f32)).T
        edge = jnp.zeros((side, 3 * lanes), bf16)
        acts[layer, 0:side, :] = edge
        acts[layer, side + length :, :] = edge
        for i in range(PIECES):
            before, same, after = shifted(activ[i * part : (i + 1) * part])
            rows = slice(side + i * part, side + (i + 1) * part)
            acts[layer, rows, 0:lanes] = before
            acts[layer, rows, lanes : 2 * lanes] = same
            acts[layer, rows, 2 * lanes :] = after

    edge = jnp.zeros((side, 3 * lanes), bf16)
    taps[0:side, :] = edge
    taps[side + length :, :] = edge
    loads[0].wait()
    for layer in range(layers):
        prepare_weights(layer)
    loads[1].wait()
    for layer in range(layers):
        prepare_state(layer)
    loads[2].wait()
    loads[3].wait()

    @pl.when(position == sections - 1)
    def _():
        incoming[...] = loss_ref[...].T

    held[...] = guess_ref[...].T

    base[...] = jnp.zeros_like(base)
    for layer in range(layers - 1, -1, -1):
        for i in range(PIECES):
            rows = slice(i * part, (i + 1) * part)
            put_taps(i * part, held[rows, :] + base[rows, :])
        for i in range(PIECES):
            rows = slice(i * part, (i + 1) * part)
            base[rows, :] += scaled[layer, rows, :] * conv(layer, i * part, part)

    @pl.when(position < sections - 1)
    def _():
        for layer in range(layers):
            prepare_acts(layer)

    neighbours = (
        groups - 1
        + (position > 0).astype(jnp.int32)
        + (position < sections - 1).astype(jnp.int32)
    )
    pl.semaphore_wait(barrier, neighbours)

    def hop(i):
        rows = pl.ds(i * size, size)
        return pltpu.make_async_remote_copy(
            src_ref=outgoing.at[rows, :],
            dst_ref=incoming.at[rows, :],
            send_sem=send_sem.at[i],
            recv_sem=recv_sem.at[i],
            device_id={"section": position - 1},
            device_id_type=MESH,
        )

    def carry(i):
        rows = slice(i * size, (i + 1) * size)
        outgoing[rows, :] = (
            incoming[rows, :] + base[rows, :]
            + layers * scaled[0, rows, :] * conv(0, i * size, size)
        )
        if i >= FLYING:
            @pl.when(position % 2 == 0)
            def _():
                hop(i - FLYING).wait_send()
        hop(i).start()

    for i in range(CHUNKS):
        @pl.when(position < sections - 1)
        def _():
            hop(i).wait_recv()

        @pl.when(position > 0)
        def _():
            rows = slice(i * size, (i + 1) * size)
            put_taps(i * size, incoming[rows, :] - held[rows, :])
            if i > 0:
                carry(i - 1)

    @pl.when(position > 0)
    def _():
        carry(CHUNKS - 1)

    @pl.when(position == sections - 1)
    def _():
        for layer in range(layers):
            prepare_acts(layer)

    def share(layer, offset):
        peer = lax.rem(member + offset, groups)
        return pltpu.make_async_remote_copy(
            src_ref=sent.at[layer, peer],
            dst_ref=landed.at[layer, offset - 1],
            send_sem=part_send.at[layer, offset - 1],
            recv_sem=part_recv.at[layer, offset - 1],
            device_id={"batch": peer},
            device_id_type=MESH,
        )

    for layer in range(layers - 1, -1, -1):
        turned_lam = incoming[...].T.astype(bf16)
        sums = []
        for a in (-1, 0, 1):
            first = side + a * side
            sums.append(
                jnp.dot(
                    turned_lam,
                    acts[layer, first : first + length, :],
                    preferred_element_type=f32,
                )
            )
        pieces = [sums[k // 3][:, (k % 3) * lanes : (k % 3 + 1) * lanes] for k in range(9)]
        held_rows = channels // groups
        for k in range(0, 9, 2):
            even = pieces[k][:channels] + pltpu.roll(pieces[k][channels:], channels, 1)
            if k < 8:
                odd = pltpu.roll(pieces[k + 1][:channels], channels, 1) + pieces[k + 1][channels:]
                both = jnp.where(low, even, odd) * STEP
                width = lanes
            else:
                both = even[:, :channels] * STEP
                width = channels
            for g in range(groups):
                share_of = both[g * held_rows : (g + 1) * held_rows]
                columns = slice(k * channels, k * channels + width)
                parts[layer, g, :, columns] = share_of
                sent[layer, g, :, columns] = share_of.astype(bf16)
        for offset in range(1, groups):
            share(layer, offset).start()

        for i in range(PIECES):
            put_taps(i * part, incoming[i * part : (i + 1) * part, :])
        for i in range(PIECES):
            rows = slice(i * part, (i + 1) * part)
            incoming[rows, :] += scaled[layer, rows, :] * conv(layer, i * part, part)

    start_ref[...] = incoming[...].T

    for layer in range(layers - 1, -1, -1):
        total = parts[layer, member]
        for offset in range(1, groups):
            share(layer, offset).wait_recv()
            total = total + landed[layer, offset - 1].astype(f32)
        grads_ref[layer] = total
        for offset in range(1, groups):
            share(layer, offset).wait_send()

    @pl.when(position % 2 == 1)
    def _():
        for i in range(CHUNKS - FLYING):
            hop(i).wait_send()

    @pl.when(position > 0)
    def _():
        for i in range(CHUNKS - FLYING, CHUNKS):
            hop(i).wait_send()


def shards(states, weights, guess, loss_cotangent):
    sections = lax.axis_size("section")
    groups = lax.axis_size("batch")
    layers, images, channels, length = states.shape
    side = math.isqrt(length)
    lanes = images * channels
    rows = channels // groups
    f32, bf16 = jnp.float32, jnp.bfloat16
    start, grads = pl.pallas_call(
        functools.partial(kernel, sections, groups, side),
        out_shape=(
            jax.ShapeDtypeStruct((lanes, length), f32),
            jax.ShapeDtypeStruct((layers, rows, 9 * channels), f32),
        ),
        in_specs=[pl.BlockSpec(memory_space=pltpu.HBM)] * 4,
        out_specs=(pl.BlockSpec(memory_space=pltpu.VMEM),) * 2,
        scratch_shapes=[
            pltpu.VMEM((layers, lanes, length), states.dtype),
            pltpu.VMEM(weights.shape, weights.dtype),
            pltpu.VMEM((lanes, length), f32),
            pltpu.VMEM((lanes, length), f32),
            pltpu.VMEM((channels, 5 * lanes), f32),
            pltpu.VMEM((layers, 9 * lanes, lanes), bf16),
            pltpu.VMEM((layers, length, lanes), f32),
            pltpu.VMEM((length, lanes), f32),
            pltpu.VMEM((length, lanes), f32),
            pltpu.VMEM((length, lanes), f32),
            pltpu.VMEM((length, lanes), f32),
            pltpu.VMEM((length + 2 * side, 3 * lanes), bf16),
            pltpu.VMEM((layers, length + 2 * side, 3 * lanes), bf16),
            pltpu.VMEM((layers, groups, rows, 9 * channels), f32),
            pltpu.VMEM((layers, groups, rows, 9 * channels), bf16),
            pltpu.VMEM((layers, groups - 1, rows, 9 * channels), bf16),
            pltpu.SemaphoreType.DMA((CHUNKS,)),
            pltpu.SemaphoreType.DMA((CHUNKS,)),
            pltpu.SemaphoreType.DMA((layers, groups - 1)),
            pltpu.SemaphoreType.DMA((layers, groups - 1)),
            pltpu.SemaphoreType.DMA((4,)),
        ],
        compiler_params=pltpu.CompilerParams(
            collective_id=0, has_side_effects=True, vmem_limit_bytes=63 * 2**20
        ),
    )(
        states.reshape(layers, lanes, length),
        weights,
        guess.reshape(lanes, length),
        loss_cotangent.reshape(lanes, length),
    )
    return start.reshape(guess.shape), grads.reshape(layers, rows * 9 * channels)


def solution(mesh):
    placed = (
        P("section", "batch", None, None),
        P("section", None, None),
        P("section", "batch", None, None),
        P("batch", None, None),
    )
    return jax.shard_map(
        shards,
        mesh=mesh,
        in_specs=placed,
        out_specs=(P("section", "batch", None, None), P("section", "batch")),
        check_vma=False,
    )
```

```python
import functools
import math

import jax
import jax.numpy as jnp
from jax import lax
from jax.experimental import pallas as pl
from jax.experimental.pallas import tpu as pltpu
from jax.sharding import PartitionSpec as P

STEP = 0.0625
PIECES = 4
CHUNKS = 8
FLYING = 2
MESH = pl.DeviceIdType.MESH


def kernel(
    sections, groups, side,
    states_hbm, weights_hbm, guess_hbm, loss_hbm, start_ref, grads_ref,
    states_ref, weights_ref, guess_ref, loss_ref,
    wide, blocks, scaled, held, base, incoming, left_over, high_in, high_out, low_in, low_out, taps, acts, parts, sent, landed,
    send_sem, recv_sem, low_send, low_recv, part_send, part_recv, load_sem,
):
    position = lax.axis_index("section")
    member = lax.axis_index("batch")
    layers = states_ref.shape[0]
    lanes, length = guess_ref.shape
    channels = weights_ref.shape[1]
    size, part = length // CHUNKS, length // PIECES
    f32, bf16 = jnp.float32, jnp.bfloat16

    loads = [
        pltpu.make_async_copy(source, target, load_sem.at[n])
        for n, (source, target) in enumerate(
            ((weights_hbm, weights_ref), (states_hbm, states_ref),
             (guess_hbm, guess_ref), (loss_hbm, loss_ref))
        )
    ]
    for load in loads:
        load.start()

    barrier = pltpu.get_barrier_semaphore()

    @pl.when(position > 0)
    def _():
        pl.semaphore_signal(
            barrier, inc=1, device_id={"section": position - 1}, device_id_type=MESH
        )

    @pl.when(position < sections - 1)
    def _():
        pl.semaphore_signal(
            barrier, inc=1, device_id={"section": position + 1}, device_id_type=MESH
        )

    for offset in range(1, groups):
        pl.semaphore_signal(
            barrier,
            inc=1,
            device_id={"batch": lax.rem(member + offset, groups)},
            device_id_type=MESH,
        )

    column = lax.broadcasted_iota(jnp.int32, (part, lanes), 0) % side
    not_first = column > 0
    not_last = column < side - 1
    low = lax.broadcasted_iota(jnp.int32, (channels, lanes), 1) < channels

    def shifted(values):
        count = values.shape[0]
        before = jnp.where(not_first[:count], pltpu.roll(values, 1, 0), 0.0)
        after = jnp.where(not_last[:count], pltpu.roll(values, count - 1, 0), 0.0)
        return before.astype(bf16), values.astype(bf16), after.astype(bf16)

    def put_taps(first, values):
        before, same, after = shifted(values)
        rows = pl.ds(first + side, values.shape[0])
        taps[rows, 0:lanes] = after
        taps[rows, lanes : 2 * lanes] = same
        taps[rows, 2 * lanes : 3 * lanes] = before

    def conv(layer, first, count):
        stacked = jnp.concatenate(
            [taps[pl.ds(first + side - a * side, count), :] for a in (-1, 0, 1)], axis=1
        )
        return jnp.dot(stacked, blocks[layer], preferred_element_type=f32)

    def prepare_weights(layer):
        wide[:, 9 * channels :] = jnp.zeros((channels, wide.shape[1] - 9 * channels), f32)
        wide[:, 0 : 9 * channels] = weights_ref[layer].astype(f32)
        for k in range(9):
            pair = wide[:, (k // 2) * lanes : (k // 2 + 1) * lanes]
            turned = pltpu.roll(pair, channels, 1)
            left, right = (pair, turned) if k % 2 == 0 else (turned, pair)
            blocks[layer, k * lanes : k * lanes + channels, :] = jnp.where(
                low, left, 0.0
            ).astype(bf16)
            blocks[layer, k * lanes + channels : (k + 1) * lanes, :] = jnp.where(
                low, 0.0, right
            ).astype(bf16)

    def prepare_state(layer):
        activ = jnp.tanh(states_ref[layer].astype(f32)).T
        scaled[layer] = STEP * (1.0 - activ * activ)

    def prepare_acts(layer):
        activ = jnp.tanh(states_ref[layer].astype(f32)).T
        edge = jnp.zeros((side, 3 * lanes), bf16)
        acts[layer, 0:side, :] = edge
        acts[layer, side + length :, :] = edge
        for i in range(PIECES):
            before, same, after = shifted(activ[i * part : (i + 1) * part])
            rows = slice(side + i * part, side + (i + 1) * part)
            acts[layer, rows, 0:lanes] = before
            acts[layer, rows, lanes : 2 * lanes] = same
            acts[layer, rows, 2 * lanes :] = after

    edge = jnp.zeros((side, 3 * lanes), bf16)
    taps[0:side, :] = edge
    taps[side + length :, :] = edge
    loads[0].wait()
    for layer in range(layers):
        prepare_weights(layer)
    loads[1].wait()
    for layer in range(layers):
        prepare_state(layer)
    loads[2].wait()
    loads[3].wait()

    @pl.when(position == sections - 1)
    def _():
        incoming[...] = loss_ref[...].T

    held[...] = guess_ref[...].T

    base[...] = jnp.zeros_like(base)
    left_over[...] = jnp.zeros_like(left_over)
    for layer in range(layers - 1, -1, -1):
        for i in range(PIECES):
            rows = slice(i * part, (i + 1) * part)
            put_taps(i * part, held[rows, :] + base[rows, :])
        for i in range(PIECES):
            rows = slice(i * part, (i + 1) * part)
            base[rows, :] += scaled[layer, rows, :] * conv(layer, i * part, part)

    @pl.when(position < sections - 1)
    def _():
        for layer in range(layers):
            prepare_acts(layer)

    neighbours = (
        groups - 1
        + (position > 0).astype(jnp.int32)
        + (position < sections - 1).astype(jnp.int32)
    )
    pl.semaphore_wait(barrier, neighbours)

    def hop(i, source=high_out, target=high_in, sends=send_sem, receives=recv_sem):
        rows = pl.ds(i * size, size)
        return pltpu.make_async_remote_copy(
            src_ref=source.at[rows, :],
            dst_ref=target.at[rows, :],
            send_sem=sends.at[i],
            recv_sem=receives.at[i],
            device_id={"section": position - 1},
            device_id_type=MESH,
        )

    def low_hop(i):
        return hop(i, low_out, low_in, low_send, low_recv)

    def carry(i):
        rows = slice(i * size, (i + 1) * size)
        value = (
            incoming[rows, :] + base[rows, :]
            + layers * scaled[0, rows, :] * conv(0, i * size, size)
        )
        high = value.astype(bf16)
        high_out[rows, :] = high
        left_over[rows, :] = value - high.astype(f32)
        if i >= FLYING:
            @pl.when(position % 2 == 0)
            def _():
                hop(i - FLYING).wait_send()
        hop(i).start()

    for i in range(CHUNKS):
        @pl.when(position < sections - 1)
        def _():
            rows = slice(i * size, (i + 1) * size)
            hop(i).wait_recv()
            incoming[rows, :] = high_in[rows, :].astype(f32)

        @pl.when(position > 0)
        def _():
            rows = slice(i * size, (i + 1) * size)
            put_taps(i * size, incoming[rows, :] - held[rows, :])
            if i > 0:
                carry(i - 1)

    @pl.when(position > 0)
    def _():
        carry(CHUNKS - 1)

    for i in range(CHUNKS):
        @pl.when(position < sections - 1)
        def _():
            rows = slice(i * size, (i + 1) * size)
            low_hop(i).wait_recv()
            low_part = low_in[rows, :].astype(f32)
            incoming[rows, :] += low_part
            left_over[rows, :] += low_part

        @pl.when(position > 0)
        def _():
            rows = slice(i * size, (i + 1) * size)
            low_out[rows, :] = left_over[rows, :].astype(bf16)
            low_hop(i).start()

    @pl.when(position == sections - 1)
    def _():
        for layer in range(layers):
            prepare_acts(layer)

    def share(layer, offset):
        peer = lax.rem(member + offset, groups)
        return pltpu.make_async_remote_copy(
            src_ref=sent.at[layer, peer],
            dst_ref=landed.at[layer, offset - 1],
            send_sem=part_send.at[layer, offset - 1],
            recv_sem=part_recv.at[layer, offset - 1],
            device_id={"batch": peer},
            device_id_type=MESH,
        )

    for layer in range(layers - 1, -1, -1):
        turned_lam = incoming[...].T.astype(bf16)
        sums = []
        for a in (-1, 0, 1):
            first = side + a * side
            sums.append(
                jnp.dot(
                    turned_lam,
                    acts[layer, first : first + length, :],
                    preferred_element_type=f32,
                )
            )
        pieces = [sums[k // 3][:, (k % 3) * lanes : (k % 3 + 1) * lanes] for k in range(9)]
        held_rows = channels // groups
        for k in range(0, 9, 2):
            even = pieces[k][:channels] + pltpu.roll(pieces[k][channels:], channels, 1)
            if k < 8:
                odd = pltpu.roll(pieces[k + 1][:channels], channels, 1) + pieces[k + 1][channels:]
                both = jnp.where(low, even, odd) * STEP
                width = lanes
            else:
                both = even[:, :channels] * STEP
                width = channels
            for g in range(groups):
                share_of = both[g * held_rows : (g + 1) * held_rows]
                columns = slice(k * channels, k * channels + width)
                parts[layer, g, :, columns] = share_of
                sent[layer, g, :, columns] = share_of.astype(bf16)
        for offset in range(1, groups):
            share(layer, offset).start()

        for i in range(PIECES):
            put_taps(i * part, incoming[i * part : (i + 1) * part, :])
        for i in range(PIECES):
            rows = slice(i * part, (i + 1) * part)
            incoming[rows, :] += scaled[layer, rows, :] * conv(layer, i * part, part)

    start_ref[...] = incoming[...].T

    for layer in range(layers - 1, -1, -1):
        total = parts[layer, member]
        for offset in range(1, groups):
            share(layer, offset).wait_recv()
            total = total + landed[layer, offset - 1].astype(f32)
        grads_ref[layer] = total
        for offset in range(1, groups):
            share(layer, offset).wait_send()

    @pl.when(position % 2 == 1)
    def _():
        for i in range(CHUNKS - FLYING):
            hop(i).wait_send()

    @pl.when(position > 0)
    def _():
        for i in range(CHUNKS - FLYING, CHUNKS):
            hop(i).wait_send()
        for i in range(CHUNKS):
            low_hop(i).wait_send()


def shards(states, weights, guess, loss_cotangent):
    sections = lax.axis_size("section")
    groups = lax.axis_size("batch")
    layers, images, channels, length = states.shape
    side = math.isqrt(length)
    lanes = images * channels
    rows = channels // groups
    f32, bf16 = jnp.float32, jnp.bfloat16
    start, grads = pl.pallas_call(
        functools.partial(kernel, sections, groups, side),
        out_shape=(
            jax.ShapeDtypeStruct((lanes, length), f32),
            jax.ShapeDtypeStruct((layers, rows, 9 * channels), f32),
        ),
        in_specs=[pl.BlockSpec(memory_space=pltpu.HBM)] * 4,
        out_specs=(pl.BlockSpec(memory_space=pltpu.VMEM),) * 2,
        scratch_shapes=[
            pltpu.VMEM((layers, lanes, length), states.dtype),
            pltpu.VMEM(weights.shape, weights.dtype),
            pltpu.VMEM((lanes, length), f32),
            pltpu.VMEM((lanes, length), f32),
            pltpu.VMEM((channels, 5 * lanes), f32),
            pltpu.VMEM((layers, 9 * lanes, lanes), bf16),
            pltpu.VMEM((layers, length, lanes), f32),
            pltpu.VMEM((length, lanes), f32),
            pltpu.VMEM((length, lanes), f32),
            pltpu.VMEM((length, lanes), f32),
            pltpu.VMEM((length, lanes), f32),
            pltpu.VMEM((length, lanes), bf16),
            pltpu.VMEM((length, lanes), bf16),
            pltpu.VMEM((length, lanes), bf16),
            pltpu.VMEM((length, lanes), bf16),
            pltpu.VMEM((length + 2 * side, 3 * lanes), bf16),
            pltpu.VMEM((layers, length + 2 * side, 3 * lanes), bf16),
            pltpu.VMEM((layers, groups, rows, 9 * channels), f32),
            pltpu.VMEM((layers, groups, rows, 9 * channels), bf16),
            pltpu.VMEM((layers, groups - 1, rows, 9 * channels), bf16),
            pltpu.SemaphoreType.DMA((CHUNKS,)),
            pltpu.SemaphoreType.DMA((CHUNKS,)),
            pltpu.SemaphoreType.DMA((CHUNKS,)),
            pltpu.SemaphoreType.DMA((CHUNKS,)),
            pltpu.SemaphoreType.DMA((layers, groups - 1)),
            pltpu.SemaphoreType.DMA((layers, groups - 1)),
            pltpu.SemaphoreType.DMA((4,)),
        ],
        compiler_params=pltpu.CompilerParams(
            collective_id=0, has_side_effects=True, vmem_limit_bytes=63 * 2**20
        ),
    )(
        states.reshape(layers, lanes, length),
        weights,
        guess.reshape(lanes, length),
        loss_cotangent.reshape(lanes, length),
    )
    return start.reshape(guess.shape), grads.reshape(layers, rows * 9 * channels)


def solution(mesh):
    placed = (
        P("section", "batch", None, None),
        P("section", None, None),
        P("section", "batch", None, None),
        P("batch", None, None),
    )
    return jax.shard_map(
        shards,
        mesh=mesh,
        in_specs=placed,
        out_specs=(P("section", "batch", None, None), P("section", "batch")),
        check_vma=False,
    )
```

```python
import functools
import math

import jax
import jax.numpy as jnp
from jax import lax
from jax.experimental import pallas as pl
from jax.experimental.pallas import tpu as pltpu
from jax.sharding import PartitionSpec as P

STEP = 0.0625
PIECES = 4
CHUNKS = 8
FLYING = 2
MESH = pl.DeviceIdType.MESH


def kernel(
    sections, groups, side,
    states_hbm, weights_hbm, guess_hbm, loss_hbm, start_ref, grads_ref,
    states_ref, weights_ref, guess_ref, loss_ref,
    wide, blocks, scaled, held, base, incoming, left_over, high_in, high_out, low_in, low_out, taps, acts, parts, sent, landed,
    send_sem, recv_sem, low_send, low_recv, part_send, part_recv, load_sem,
):
    position = lax.axis_index("section")
    member = lax.axis_index("batch")
    layers = states_ref.shape[0]
    lanes, length = guess_ref.shape
    channels = weights_ref.shape[1]
    size, part = length // CHUNKS, length // PIECES
    f32, bf16 = jnp.float32, jnp.bfloat16

    loads = [
        pltpu.make_async_copy(source, target, load_sem.at[n])
        for n, (source, target) in enumerate(
            ((weights_hbm, weights_ref), (states_hbm, states_ref),
             (guess_hbm, guess_ref), (loss_hbm, loss_ref))
        )
    ]
    for load in loads:
        load.start()

    barrier = pltpu.get_barrier_semaphore()

    @pl.when(position > 0)
    def _():
        pl.semaphore_signal(
            barrier, inc=1, device_id={"section": position - 1}, device_id_type=MESH
        )

    @pl.when(position < sections - 1)
    def _():
        pl.semaphore_signal(
            barrier, inc=1, device_id={"section": position + 1}, device_id_type=MESH
        )

    for offset in range(1, groups):
        pl.semaphore_signal(
            barrier,
            inc=1,
            device_id={"batch": lax.rem(member + offset, groups)},
            device_id_type=MESH,
        )

    column = lax.broadcasted_iota(jnp.int32, (part, lanes), 0) % side
    not_first = column > 0
    not_last = column < side - 1
    low = lax.broadcasted_iota(jnp.int32, (channels, lanes), 1) < channels

    def shifted(values):
        count = values.shape[0]
        before = jnp.where(not_first[:count], pltpu.roll(values, 1, 0), 0.0)
        after = jnp.where(not_last[:count], pltpu.roll(values, count - 1, 0), 0.0)
        return before.astype(bf16), values.astype(bf16), after.astype(bf16)

    def put_taps(first, values):
        before, same, after = shifted(values)
        rows = pl.ds(first + side, values.shape[0])
        taps[rows, 0:lanes] = after
        taps[rows, lanes : 2 * lanes] = same
        taps[rows, 2 * lanes : 3 * lanes] = before

    def conv(layer, first, count):
        stacked = jnp.concatenate(
            [taps[pl.ds(first + side - a * side, count), :] for a in (-1, 0, 1)], axis=1
        )
        return jnp.dot(stacked, blocks[layer], preferred_element_type=f32)

    def prepare_weights(layer):
        wide[:, 9 * channels :] = jnp.zeros((channels, wide.shape[1] - 9 * channels), f32)
        wide[:, 0 : 9 * channels] = weights_ref[layer].astype(f32)
        for k in range(9):
            pair = wide[:, (k // 2) * lanes : (k // 2 + 1) * lanes]
            turned = pltpu.roll(pair, channels, 1)
            left, right = (pair, turned) if k % 2 == 0 else (turned, pair)
            blocks[layer, k * lanes : k * lanes + channels, :] = jnp.where(
                low, left, 0.0
            ).astype(bf16)
            blocks[layer, k * lanes + channels : (k + 1) * lanes, :] = jnp.where(
                low, 0.0, right
            ).astype(bf16)

    def prepare_state(layer):
        activ = jnp.tanh(states_ref[layer].astype(f32)).T
        scaled[layer] = STEP * (1.0 - activ * activ)

    def prepare_acts(layer):
        activ = jnp.tanh(states_ref[layer].astype(f32)).T
        edge = jnp.zeros((side, 3 * lanes), bf16)
        acts[layer, 0:side, :] = edge
        acts[layer, side + length :, :] = edge
        for i in range(PIECES):
            before, same, after = shifted(activ[i * part : (i + 1) * part])
            rows = slice(side + i * part, side + (i + 1) * part)
            acts[layer, rows, 0:lanes] = before
            acts[layer, rows, lanes : 2 * lanes] = same
            acts[layer, rows, 2 * lanes :] = after

    edge = jnp.zeros((side, 3 * lanes), bf16)
    taps[0:side, :] = edge
    taps[side + length :, :] = edge
    loads[0].wait()
    for layer in range(layers):
        prepare_weights(layer)
    loads[1].wait()
    for layer in range(layers):
        prepare_state(layer)
    loads[2].wait()
    loads[3].wait()

    @pl.when(position == sections - 1)
    def _():
        incoming[...] = loss_ref[...].T

    held[...] = guess_ref[...].T

    base[...] = jnp.zeros_like(base)
    left_over[...] = jnp.zeros_like(left_over)
    for layer in range(layers - 1, -1, -1):
        for i in range(PIECES):
            rows = slice(i * part, (i + 1) * part)
            put_taps(i * part, held[rows, :] + base[rows, :])
        for i in range(PIECES):
            rows = slice(i * part, (i + 1) * part)
            base[rows, :] += scaled[layer, rows, :] * conv(layer, i * part, part)

    @pl.when(position < sections - 1)
    def _():
        for layer in range(layers):
            prepare_acts(layer)

    neighbours = (
        groups - 1
        + (position > 0).astype(jnp.int32)
        + (position < sections - 1).astype(jnp.int32)
    )
    pl.semaphore_wait(barrier, neighbours)

    def hop(i, source=high_out, target=high_in, sends=send_sem, receives=recv_sem):
        rows = pl.ds(i * size, size)
        return pltpu.make_async_remote_copy(
            src_ref=source.at[rows, :],
            dst_ref=target.at[rows, :],
            send_sem=sends.at[i],
            recv_sem=receives.at[i],
            device_id={"section": position - 1},
            device_id_type=MESH,
        )

    def low_hop(i):
        return hop(i, low_out, low_in, low_send, low_recv)

    def carry(i):
        rows = slice(i * size, (i + 1) * size)
        value = (
            incoming[rows, :] + base[rows, :]
            + layers * scaled[0, rows, :] * conv(0, i * size, size)
        )
        high = value.astype(bf16)
        high_out[rows, :] = high
        left_over[rows, :] = value - high.astype(f32)
        if i >= FLYING:
            @pl.when(position % 2 == 0)
            def _():
                hop(i - FLYING).wait_send()
        hop(i).start()

    for i in range(CHUNKS):
        @pl.when(position < sections - 1)
        def _():
            rows = slice(i * size, (i + 1) * size)
            hop(i).wait_recv()
            incoming[rows, :] = high_in[rows, :].astype(f32)

        @pl.when(position > 0)
        def _():
            rows = slice(i * size, (i + 1) * size)
            put_taps(i * size, incoming[rows, :] - held[rows, :])
            if i > 0:
                carry(i - 1)

    @pl.when(position > 0)
    def _():
        carry(CHUNKS - 1)

    for i in range(CHUNKS):
        @pl.when(position < sections - 1)
        def _():
            rows = slice(i * size, (i + 1) * size)
            low_hop(i).wait_recv()
            low_part = low_in[rows, :].astype(f32)
            incoming[rows, :] += low_part
            left_over[rows, :] += low_part

        @pl.when(position > 0)
        def _():
            rows = slice(i * size, (i + 1) * size)
            low_out[rows, :] = left_over[rows, :].astype(bf16)
            if i >= FLYING:
                @pl.when(position % 2 == 0)
                def _():
                    low_hop(i - FLYING).wait_send()
            low_hop(i).start()

    @pl.when(position == sections - 1)
    def _():
        for layer in range(layers):
            prepare_acts(layer)

    def share(layer, offset):
        peer = lax.rem(member + offset, groups)
        return pltpu.make_async_remote_copy(
            src_ref=sent.at[layer, peer],
            dst_ref=landed.at[layer, offset - 1],
            send_sem=part_send.at[layer, offset - 1],
            recv_sem=part_recv.at[layer, offset - 1],
            device_id={"batch": peer},
            device_id_type=MESH,
        )

    for layer in range(layers - 1, -1, -1):
        turned_lam = incoming[...].T.astype(bf16)
        sums = []
        for a in (-1, 0, 1):
            first = side + a * side
            sums.append(
                jnp.dot(
                    turned_lam,
                    acts[layer, first : first + length, :],
                    preferred_element_type=f32,
                )
            )
        pieces = [sums[k // 3][:, (k % 3) * lanes : (k % 3 + 1) * lanes] for k in range(9)]
        held_rows = channels // groups
        for k in range(0, 9, 2):
            even = pieces[k][:channels] + pltpu.roll(pieces[k][channels:], channels, 1)
            if k < 8:
                odd = pltpu.roll(pieces[k + 1][:channels], channels, 1) + pieces[k + 1][channels:]
                both = jnp.where(low, even, odd) * STEP
                width = lanes
            else:
                both = even[:, :channels] * STEP
                width = channels
            for g in range(groups):
                share_of = both[g * held_rows : (g + 1) * held_rows]
                columns = slice(k * channels, k * channels + width)
                parts[layer, g, :, columns] = share_of
                sent[layer, g, :, columns] = share_of.astype(bf16)
        for offset in range(1, groups):
            share(layer, offset).start()

        for i in range(PIECES):
            put_taps(i * part, incoming[i * part : (i + 1) * part, :])
        for i in range(PIECES):
            rows = slice(i * part, (i + 1) * part)
            incoming[rows, :] += scaled[layer, rows, :] * conv(layer, i * part, part)

    start_ref[...] = incoming[...].T

    for layer in range(layers - 1, -1, -1):
        total = parts[layer, member]
        for offset in range(1, groups):
            share(layer, offset).wait_recv()
            total = total + landed[layer, offset - 1].astype(f32)
        grads_ref[layer] = total
        for offset in range(1, groups):
            share(layer, offset).wait_send()

    @pl.when(position % 2 == 1)
    def _():
        for i in range(CHUNKS - FLYING):
            hop(i).wait_send()
            low_hop(i).wait_send()

    @pl.when(position > 0)
    def _():
        for i in range(CHUNKS - FLYING, CHUNKS):
            hop(i).wait_send()
            low_hop(i).wait_send()


def shards(states, weights, guess, loss_cotangent):
    sections = lax.axis_size("section")
    groups = lax.axis_size("batch")
    layers, images, channels, length = states.shape
    side = math.isqrt(length)
    lanes = images * channels
    rows = channels // groups
    f32, bf16 = jnp.float32, jnp.bfloat16
    start, grads = pl.pallas_call(
        functools.partial(kernel, sections, groups, side),
        out_shape=(
            jax.ShapeDtypeStruct((lanes, length), f32),
            jax.ShapeDtypeStruct((layers, rows, 9 * channels), f32),
        ),
        in_specs=[pl.BlockSpec(memory_space=pltpu.HBM)] * 4,
        out_specs=(pl.BlockSpec(memory_space=pltpu.VMEM),) * 2,
        scratch_shapes=[
            pltpu.VMEM((layers, lanes, length), states.dtype),
            pltpu.VMEM(weights.shape, weights.dtype),
            pltpu.VMEM((lanes, length), f32),
            pltpu.VMEM((lanes, length), f32),
            pltpu.VMEM((channels, 5 * lanes), f32),
            pltpu.VMEM((layers, 9 * lanes, lanes), bf16),
            pltpu.VMEM((layers, length, lanes), f32),
            pltpu.VMEM((length, lanes), f32),
            pltpu.VMEM((length, lanes), f32),
            pltpu.VMEM((length, lanes), f32),
            pltpu.VMEM((length, lanes), f32),
            pltpu.VMEM((length, lanes), bf16),
            pltpu.VMEM((length, lanes), bf16),
            pltpu.VMEM((length, lanes), bf16),
            pltpu.VMEM((length, lanes), bf16),
            pltpu.VMEM((length + 2 * side, 3 * lanes), bf16),
            pltpu.VMEM((layers, length + 2 * side, 3 * lanes), bf16),
            pltpu.VMEM((layers, groups, rows, 9 * channels), f32),
            pltpu.VMEM((layers, groups, rows, 9 * channels), bf16),
            pltpu.VMEM((layers, groups - 1, rows, 9 * channels), bf16),
            pltpu.SemaphoreType.DMA((CHUNKS,)),
            pltpu.SemaphoreType.DMA((CHUNKS,)),
            pltpu.SemaphoreType.DMA((CHUNKS,)),
            pltpu.SemaphoreType.DMA((CHUNKS,)),
            pltpu.SemaphoreType.DMA((layers, groups - 1)),
            pltpu.SemaphoreType.DMA((layers, groups - 1)),
            pltpu.SemaphoreType.DMA((4,)),
        ],
        compiler_params=pltpu.CompilerParams(
            collective_id=0, has_side_effects=True, vmem_limit_bytes=63 * 2**20
        ),
    )(
        states.reshape(layers, lanes, length),
        weights,
        guess.reshape(lanes, length),
        loss_cotangent.reshape(lanes, length),
    )
    return start.reshape(guess.shape), grads.reshape(layers, rows * 9 * channels)


def solution(mesh):
    placed = (
        P("section", "batch", None, None),
        P("section", None, None),
        P("section", "batch", None, None),
        P("batch", None, None),
    )
    return jax.shard_map(
        shards,
        mesh=mesh,
        in_specs=placed,
        out_specs=(P("section", "batch", None, None), P("section", "batch")),
        check_vma=False,
    )
```
